32 devices in a mesh: group: 2 (over y), expert: 4 (over z), dp: 4 (over x, core).
Axes of the slice: x: 2, y: 2, z: 4, core: 2. Of those that a mesh axis runs over, the one named last changes fastest.
Arguments:
- tokens: bfloat16 [1536, 6144], P(('group', 'expert'), 'dp'), parts along dimension 0, may hold values from -6 to 6
- out_grad: bfloat16 [1536, 6144], P(('group', 'expert'), 'dp'), parts along dimension 0, may hold values from -0.59765625 to 0.59765625
- gate_probs: float32 [1536, 4], P(('group', 'expert')), parts along dimension 0, may hold values from 0.1 to 1
- routes: int32 [1536, 4], P(('group', 'expert')), parts along dimension 0, may hold values from 0 to 15, as said below
- expert_weights: bfloat16 [3, 10752, 6144], P(None, 'expert', 'dp'), may hold values from -0.078125 to 0.078125
Outputs:
- weight_grads: float32 [6, 10752, 6144], P('group', 'expert', 'dp'), parts along dimension 0
The draws below stay inside these ranges and needn't reach their ends.
There are 2 independent parts, one for each index of `group`. The reference program is written for one: setup_inputs(seed, part) draws one part's arguments, and reference() takes and returns one part's arrays. A program takes and returns all parts, laid end to end along the dimension named above; an argument that names none is the same for every part. Nothing has to cross between parts.
Inputs may be any that keep to these rules, and one draw needn't show every extreme that they name: `routes`: each row names 4 different experts. Among the 192 rows held by one device along `expert`, expert 0 is named by at most 48 rows, and in every draw some device along `expert` has exactly 48 such rows.
All inputs are finite; a program needn't handle non-finite values.
Results may differ from the reference program's by a relative error of at most 0.0041.
Values may be sent and summed in bfloat16 or wider, within the bound.
No kernel may reach another device: no remote copies, remote signals or barrier semaphores. Data moves between devices by JAX's collectives and lax.ppermute only.
A program may use at most 256 MiB of HBM per device.

```python
import jax
import jax.numpy as jnp
from jax import lax

D = 6144
HID = 10752
EXPERTS = 16
TOP = 4
TOK_GRP = 192
CAP = 48
TOKENS = 768
N_EXPERT = 4


def draw_routes(key, part):
    key = jax.random.fold_in(key, 11)
    keys = jax.random.split(key, 5)
    others_n = EXPERTS - 1
    bits = jax.random.randint(keys[0], (TOKENS, others_n), 0, 2 ** 20)
    scores = bits * EXPERTS + jnp.arange(others_n, dtype=jnp.int32)[None, :]
    picked = lax.top_k(scores, TOP)[1].astype(jnp.int32) + 1
    counts = jax.random.randint(keys[1], (N_EXPERT,), CAP // 4, CAP // 2 + 1)
    busiest = jax.random.randint(keys[2], (), 0, N_EXPERT)
    counts = jnp.where(jnp.arange(N_EXPERT, dtype=jnp.int32) == busiest, CAP, counts).astype(jnp.int32)
    prio = jax.random.randint(keys[3], (N_EXPERT, TOK_GRP), 0, 2 ** 20) * TOK_GRP + jnp.arange(TOK_GRP, dtype=jnp.int32)[None, :]
    order = jnp.argsort(jnp.argsort(prio, axis=1, stable=True), axis=1, stable=True).astype(jnp.int32)
    chosen = (order < counts[:, None]).reshape(TOKENS)
    which = jax.random.randint(keys[4], (TOKENS,), 0, TOP)
    place = chosen[:, None] & (jnp.arange(TOP, dtype=jnp.int32)[None, :] == which[:, None])
    return jnp.where(place, 0, picked).astype(jnp.int32)


def level_of(rng, dims, shards, smallest, top_value):
    factor_of = 1.0
    for position, parts in shards:
        heights = jax.random.uniform(jax.random.fold_in(jax.random.fold_in(rng, 6), position), (parts,), jnp.float32, smallest / len(shards), top_value / len(shards))
        factor_of = factor_of * jnp.repeat(jnp.exp(heights), dims[position] // parts).reshape((-1,) + (1,) * (len(dims) - 1 - position))
    return factor_of


def bell_draw(own_key, extent, scale, most, shards=(), kind=jnp.bfloat16):
    drawn = jax.random.normal(own_key, extent, jnp.float32) * scale
    if len(shards) > 0:
        drawn = level_of(own_key, extent, shards, -0.22, 0.18) * drawn
    return jnp.clip(drawn, min=-most, max=most).astype(kind)


def setup_inputs(seed: int = 0, part: int = 0) -> dict:
    streams_of = jax.random.split(jax.random.key(seed), 6)
    part_keys = jax.random.split(jax.random.fold_in(streams_of[5], part), 6)
    tokens = bell_draw(part_keys[0], (TOKENS, D), 1.0, 6.0, ((0, 4), (1, 4)))
    out_grad = bell_draw(part_keys[1], (TOKENS, D), 0.1, 0.59765625, ((0, 4), (1, 4)))
    gate_probs = jnp.clip(0.1 + 0.9 * jax.random.uniform(part_keys[2], (TOKENS, TOP), jnp.float32) ** level_of(part_keys[2], (TOKENS, TOP), ((0, 4),), -0.2, 0.2), 0.1, 1.0)
    routes = draw_routes(jax.random.fold_in(jax.random.fold_in(streams_of[5], part), 71), part)
    expert_weights = bell_draw(streams_of[4], (3, HID, D), D ** -0.5, 0.078125, ((1, 4), (2, 4)))
    return dict(tokens=tokens, out_grad=out_grad, gate_probs=gate_probs, routes=routes, expert_weights=expert_weights)


def activations(gate_up, down_grad, width):
    gate = gate_up[:, :width]
    up = gate_up[:, width:]
    sig = jax.nn.sigmoid(gate)
    hidden = (gate * sig * up).astype(jnp.bfloat16)
    gate_grad = down_grad * up * sig * (1.0 + gate * (1.0 - sig))
    up_grad = down_grad * gate * sig
    left = jnp.concatenate([gate_grad, up_grad], axis=1).astype(jnp.bfloat16)
    return left, hidden


def reference(tokens, out_grad, gate_probs, routes, expert_weights):
    bound = N_EXPERT * CAP
    hit = routes == 0
    token_hit = jnp.any(hit, axis=1)
    prob = jnp.sum(jnp.where(hit, gate_probs, jnp.zeros_like(gate_probs)), axis=1)
    index = jnp.nonzero(token_hit, size=bound, fill_value=TOKENS)[0].astype(jnp.int32)
    padded_tokens = jnp.concatenate([tokens, jnp.zeros((1, D), jnp.bfloat16)], axis=0)
    padded_grad = jnp.concatenate([out_grad, jnp.zeros((1, D), jnp.bfloat16)], axis=0)
    padded_prob = jnp.concatenate([prob, jnp.zeros((1,), jnp.float32)], axis=0)
    rows_x = padded_tokens[index]
    rows_dy = (padded_grad[index].astype(jnp.float32) * padded_prob[index][:, None]).astype(jnp.bfloat16)
    w_gateup = expert_weights[:2].reshape(2 * HID, D)
    gate_up = jnp.dot(rows_x, w_gateup.T, preferred_element_type=jnp.float32)
    down_grad = jnp.dot(rows_dy, expert_weights[2].T, preferred_element_type=jnp.float32)
    left, hidden = activations(gate_up, down_grad, HID)
    part_gu = jnp.dot(left.T, rows_x, preferred_element_type=jnp.float32)
    part_down = jnp.dot(hidden.T, rows_dy, preferred_element_type=jnp.float32)
    return jnp.concatenate([part_gu, part_down], axis=0).reshape(3, HID, D)
```

```python
import functools

import jax
import jax.numpy as jnp
from jax import lax
from jax.experimental import pallas as pl
from jax.experimental.pallas import tpu as pltpu
from jax.sharding import PartitionSpec as P

STEP = 384
REST_CHUNKS = (2, 2, 2, 1)
VMEM = 24 * 1024 * 1024
SMALL = 8 * 1024 * 1024
FLOPS = 10**10


def contract_last(left, right):
    return lax.dot_general(
        left, right, (((1,), (1,)), ((), ())), preferred_element_type=jnp.float32
    )


def contract_first(left, right):
    return lax.dot_general(
        left, right, (((0,), (0,)), ((), ())), preferred_element_type=jnp.float32
    )


def activations(gate, up, down_grad):
    sig = jax.nn.sigmoid(gate)
    hidden = gate * sig * up
    gate_grad = down_grad * up * sig * (1.0 + gate * (1.0 - sig))
    up_grad = down_grad * gate * sig
    return jnp.stack([gate_grad, up_grad, hidden]).astype(jnp.bfloat16)


def pick_rows(tokens, out_grad, gate_probs, routes, flip):
    capacity = tokens.shape[0] // 4
    hit = routes == 0
    token_hit = jnp.any(hit, axis=1)
    prob = jnp.sum(jnp.where(hit, gate_probs, jnp.zeros_like(gate_probs)), axis=1)
    flags = token_hit.astype(jnp.int32)
    before = jnp.cumsum(flags, dtype=jnp.int32) - flags
    place = jnp.arange(capacity, dtype=jnp.int32)
    place = jnp.where(flip, lax.rem(place + capacity // 2, capacity), place)
    match = token_hit[None, :] & (before[None, :] == place[:, None])
    picker = match.astype(jnp.bfloat16)
    scaled = (out_grad.astype(jnp.float32) * prob[:, None]).astype(jnp.bfloat16)
    rows_x = jnp.dot(picker, tokens, preferred_element_type=jnp.float32).astype(jnp.bfloat16)
    rows_dy = jnp.dot(picker, scaled, preferred_element_type=jnp.float32).astype(jnp.bfloat16)
    return jnp.stack([rows_x, rows_dy])


def call(kernel, name, args, in_specs, out_specs, out_shape, after=(), grid=(), aliases=None, vmem=SMALL, flops=1000):
    return pl.pallas_call(
        kernel,
        grid=grid,
        in_specs=list(in_specs) + [pl.BlockSpec(memory_space=pl.ANY)] * len(after),
        out_specs=out_specs,
        out_shape=out_shape,
        input_output_aliases=aliases or {},
        compiler_params=pltpu.CompilerParams(vmem_limit_bytes=vmem),
        cost_estimate=pl.CostEstimate(flops=flops, bytes_accessed=1000, transcendentals=0),
        name=name,
    )(*args, *after)


def own_kernel(rows_ref, w_ref, own_ref, send_ref, kept_ref, sems):
    half = own_ref.shape[1]
    steps = kept_ref.shape[1] // STEP

    def piece(i):
        here = pl.ds(pl.multiple_of(i * STEP, STEP), STEP)
        return pltpu.make_async_copy(w_ref.at[:, here, :], kept_ref.at[:, here, :], sems.at[i])

    for i in range(steps):
        piece(i).start()

    def step(i, carry):
        piece(i).wait()
        here = pl.ds(pl.multiple_of(i * STEP, STEP), STEP)
        w = kept_ref[:, here, :]
        gate_up = contract_last(rows_ref[0], w[:2].reshape(2 * STEP, w.shape[2]))
        down = contract_last(rows_ref[1], w[2])
        for m, part in enumerate((gate_up[:, :STEP], gate_up[:, STEP:], down)):
            own_ref[m, :, here] = part[:half]
            send_ref[m, :, here] = part[half:].astype(jnp.bfloat16)
        return carry

    lax.fori_loop(0, steps, step, 0)


def forward_own(rows, weights):
    half, hid = rows.shape[1] // 2, weights.shape[1]
    return pl.pallas_call(
        own_kernel,
        in_specs=[pl.BlockSpec(memory_space=pltpu.VMEM), pl.BlockSpec(memory_space=pl.ANY)],
        out_specs=[pl.BlockSpec(memory_space=pltpu.VMEM)] * 3,
        out_shape=[
            jax.ShapeDtypeStruct((3, half, hid), jnp.float32),
            jax.ShapeDtypeStruct((3, half, hid), jnp.bfloat16),
            pltpu.VMEM(weights.shape, weights.dtype),
        ],
        scratch_shapes=[pltpu.SemaphoreType.DMA((hid // STEP,))],
        compiler_params=pltpu.CompilerParams(vmem_limit_bytes=SMALL),
        cost_estimate=pl.CostEstimate(flops=1000, bytes_accessed=1000, transcendentals=0),
        name="forward_own",
    )(rows, weights)


def forward_kernel(first, top, rows_ref, w_ref, *refs):
    own_ref, send_ref = refs[-2:]
    half, step = own_ref.shape[1:]
    start = pl.multiple_of((first + pl.program_id(0)) * step, step)
    w = w_ref[:, pl.ds(start, step), :]
    gate_up = contract_last(rows_ref[0, top:, :], w[:2].reshape(2 * step, w.shape[2]))
    down = contract_last(rows_ref[1, top:, :], w[2])
    for m, part in enumerate((gate_up[:, :step], gate_up[:, step:], down)):
        own_ref[m] = part[:half]
        send_ref[m] = part[half:].astype(jnp.bfloat16)


def forward(rows, top, weights, first, steps, after):
    _, count, width = rows.shape
    half, chunk = (count - top) // 2, steps * STEP
    return call(
        functools.partial(forward_kernel, first, top),
        "forward",
        (rows, weights),
        [
            pl.BlockSpec((2, count, width), lambda i: (0, 0, 0)),
            pl.BlockSpec(memory_space=pltpu.VMEM),
        ],
        [pl.BlockSpec((3, half, STEP), lambda i: (0, 0, i))] * 2,
        [
            jax.ShapeDtypeStruct((3, half, chunk), jnp.float32),
            jax.ShapeDtypeStruct((3, half, chunk), jnp.bfloat16),
        ],
        after,
        (steps,),
        flops=FLOPS,
    )


def backward_kernel(a_ref, b_ref, c_ref, d_ref, rows_ref, *refs):
    out_ref = refs[-1]
    for m in range(3):
        parts = [ref[m].astype(jnp.float32) for ref in (a_ref, b_ref, c_ref, d_ref)]
        left = jnp.concatenate(parts, axis=0).astype(jnp.bfloat16)
        out_ref[m] = contract_first(left, rows_ref[m // 2])


def backward(lefts, rows, grads, shape, first, steps, after):
    _, count, width = rows.shape
    in_specs = [
        pl.BlockSpec(
            (3, v.shape[1], STEP), lambda i, k=first if v.shape[2] == shape[1] else 0: (0, 0, k + i)
        )
        for v in lefts
    ] + [pl.BlockSpec((2, count, width), lambda i: (0, 0, 0))]
    args, aliases = list(lefts) + [rows], {}
    if grads is not None:
        after, aliases = (grads,) + after, {len(args): 0}
    return call(
        backward_kernel,
        "backward",
        args,
        in_specs,
        pl.BlockSpec((3, STEP, width), lambda i: (0, first + i, 0)),
        jax.ShapeDtypeStruct(shape, jnp.float32),
        after,
        (steps,),
        aliases,
        VMEM,
    )


def add_kernel(own_ref, received_ref, *refs):
    total = own_ref[...] + received_ref[...].astype(jnp.float32)
    refs[-2][...] = total
    refs[-1][...] = total.astype(jnp.bfloat16)


def act_kernel(pieces, *refs):
    left_ref, start = refs[-1], 0
    for k in range(pieces):
        total_ref, received_ref = refs[2 * k : 2 * k + 2]
        here = slice(start, start + total_ref.shape[2])
        start += total_ref.shape[2]
        gate, up, down_grad = [total_ref[m] + received_ref[m].astype(jnp.float32) for m in range(3)]
        sig = jax.nn.sigmoid(gate)
        left_ref[0, :, here] = (down_grad * up * sig * (1.0 + gate * (1.0 - sig))).astype(jnp.bfloat16)
        left_ref[1, :, here] = (down_grad * gate * sig).astype(jnp.bfloat16)
        left_ref[2, :, here] = (gate * sig * up).astype(jnp.bfloat16)


def add(own, received, after):
    whole = [pl.BlockSpec(memory_space=pltpu.VMEM)] * 2
    shapes = [jax.ShapeDtypeStruct(own.shape, t) for t in (jnp.float32, jnp.bfloat16)]
    return call(add_kernel, "add", (own, received), whole, whole, shapes, after)


def activate(sums, after):
    whole = pl.BlockSpec(memory_space=pltpu.VMEM)
    args = [v for pair in sums for v in pair]
    three, half, _ = args[0].shape
    shape = jax.ShapeDtypeStruct((three, half, sum(v.shape[2] for v, _ in sums)), jnp.bfloat16)
    kernel = functools.partial(act_kernel, len(sums))
    return call(kernel, "activate", args, [whole] * len(args), whole, shape, after)


def arrange_kernel(own_ref, lower_ref, upper_ref, far_lower_ref, far_upper_ref, *refs):
    rows_ref = refs[-1]
    half = own_ref.shape[1] // 2
    for m in range(2):
        lower, upper, one, other = [
            ref[m].astype(jnp.float32) for ref in (lower_ref, upper_ref, far_lower_ref, far_upper_ref)
        ]
        far = one + other
        parts = [own_ref[m].astype(jnp.float32), lower[:half], upper[:half], far[:half]]
        parts += [lower[half:], upper[half:], far[half:]]
        rows_ref[m] = jnp.concatenate(parts, axis=0).astype(jnp.bfloat16)


def arrange(blocks, after):
    whole = pl.BlockSpec(memory_space=pltpu.VMEM)
    two, count, width = blocks[0].shape
    shape = jax.ShapeDtypeStruct((two, 4 * count, width), jnp.bfloat16)
    return call(arrange_kernel, "arrange", blocks, [whole] * 5, whole, shape, after)


def to_core(v):
    return lax.ppermute(v, "dp", [(i, i ^ 1) for i in range(4)])


def to_chip(v):
    return lax.ppermute(v, "dp", [(i, i ^ 2) for i in range(4)])


def forward_all(rows, top, weights, chunks, last, between):
    first, firsts = 0, []
    for steps in chunks:
        firsts.append(first)
        first += steps
    parts, sums = [], []
    for k in range(len(chunks) + 1):
        if k < len(chunks):
            own, send = forward(rows, top, weights, firsts[k], chunks[k], last)
            parts.append((own, to_core(send)))
            last = (own,)
        if k == 0:
            left = between(last)
            last = (left,)
        if k >= 1:
            total, sent = add(*parts[k - 1], last)
            sums.append((total, to_chip(sent)))
            last = (total,)
    return sums, left, last


def pipeline(block, weights):
    lower = lax.ppermute(block, "expert", [(i, (i + 1) % 4) for i in range(4)])
    upper = lax.ppermute(block, "expert", [(i, (i - 1) % 4) for i in range(4)])
    own, send, resident = forward_own(block, weights)
    lower_out, _ = lax.optimization_barrier((lower, own))
    far_lower = lax.ppermute(lower_out, "expert", [(1, 2), (2, 3)])
    far_upper = lax.ppermute(upper, "expert", [(2, 1), (1, 0)])
    total, sent = add(own, to_core(send), ())
    own_sums, last = [(total, to_chip(sent))], (total,)
    rows = arrange([block, lower, upper, far_lower, far_upper], last)
    sums, left, last = forward_all(
        rows, block.shape[1], resident, REST_CHUNKS, (rows,), functools.partial(activate, own_sums)
    )
    own_left = [left, to_core(left)]
    grads, first, lefts = None, 0, []
    for k in range(len(sums) + 1):
        if k < len(sums):
            left = activate([sums[k]], last)
            lefts.append([left, to_core(left)])
            last = (left,)
        if k >= 1:
            after = last if k < len(sums) else ()
            grads = backward(
                own_left + lefts[k - 1], rows, grads, weights.shape, first, REST_CHUNKS[k - 1], after
            )
            first += REST_CHUNKS[k - 1]
            last = (grads,)
    return grads


def fallback(block, weights):
    moved = lax.all_gather(block, "expert", axis=1, tiled=True)
    _, hid, width = weights.shape
    gate_up = contract_last(moved[0], weights[:2].reshape(2 * hid, width))
    down = contract_last(moved[1], weights[2])
    total = lax.psum(jnp.concatenate([gate_up, down], axis=1), "dp")
    left = activations(total[:, :hid], total[:, hid : 2 * hid], total[:, 2 * hid :])
    return jnp.stack(
        [
            contract_first(left[0], moved[0]),
            contract_first(left[1], moved[0]),
            contract_first(left[2], moved[1]),
        ]
    )


def per_device(n_expert, n_dp, tokens, out_grad, gate_probs, routes, weights):
    hid = weights.shape[1]
    if n_expert == 4 and n_dp == 4 and hid == STEP * sum(REST_CHUNKS) and tokens.shape[0] % 64 == 0:
        flip = lax.rem(lax.axis_index("dp"), 2) == 1
        return pipeline(pick_rows(tokens, out_grad, gate_probs, routes, flip), weights)
    return fallback(pick_rows(tokens, out_grad, gate_probs, routes, False), weights)


def solution(mesh):
    in_specs = (
        P(("group", "expert"), "dp"),
        P(("group", "expert"), "dp"),
        P(("group", "expert"), None),
        P(("group", "expert"), None),
        P(None, "expert", "dp"),
    )
    out_specs = P("group", "expert", "dp")
    step = functools.partial(per_device, mesh.shape["expert"], mesh.shape["dp"])
    return jax.shard_map(
        step, mesh=mesh, in_specs=in_specs, out_specs=out_specs, check_vma=False
    )
```

```python
import functools

import jax
import jax.numpy as jnp
from jax import lax
from jax.experimental import pallas as pl
from jax.experimental.pallas import tpu as pltpu
from jax.sharding import PartitionSpec as P

STEP = 384
BACK_BLOCKS = (256, 384)
REST_CHUNKS = (2, 3, 2)
AHEAD = (1, 2, 3)
DEFER = 1
VMEM = 24 * 1024 * 1024
SMALL = 8 * 1024 * 1024
LARGE = 253 * 256 * 1024
FLOPS = 4 * 10**9
BACK_FLOPS = 1000
FINAL_FLOPS = 5*10**9


def contract_last(left, right):
    return lax.dot_general(
        left, right, (((1,), (1,)), ((), ())), preferred_element_type=jnp.float32
    )


def contract_first(left, right):
    return lax.dot_general(
        left, right, (((0,), (0,)), ((), ())), preferred_element_type=jnp.float32
    )


def activations(gate, up, down_grad):
    sig = jax.nn.sigmoid(gate)
    hidden = gate * sig * up
    gate_grad = down_grad * up * sig * (1.0 + gate * (1.0 - sig))
    up_grad = down_grad * gate * sig
    return jnp.stack([gate_grad, up_grad, hidden]).astype(jnp.bfloat16)


def pick_rows(tokens, out_grad, gate_probs, routes):
    capacity = tokens.shape[0] // 4
    hit = routes == 0
    token_hit = jnp.any(hit, axis=1)
    prob = jnp.sum(jnp.where(hit, gate_probs, jnp.zeros_like(gate_probs)), axis=1)
    flags = token_hit.astype(jnp.int32)
    before = jnp.cumsum(flags, dtype=jnp.int32) - flags
    place = jnp.arange(capacity, dtype=jnp.int32)
    match = token_hit[None, :] & (before[None, :] == place[:, None])
    picker = match.astype(jnp.bfloat16)
    scaled = (out_grad.astype(jnp.float32) * prob[:, None]).astype(jnp.bfloat16)
    rows_x = jnp.dot(picker, tokens, preferred_element_type=jnp.float32).astype(jnp.bfloat16)
    rows_dy = jnp.dot(picker, scaled, preferred_element_type=jnp.float32).astype(jnp.bfloat16)
    return jnp.stack([rows_x, rows_dy])


def call(kernel, name, args, in_specs, out_specs, out_shape, after=(), grid=(), aliases=None, vmem=SMALL, flops=1000):
    return pl.pallas_call(
        kernel,
        grid=grid,
        in_specs=list(in_specs) + [pl.BlockSpec(memory_space=pl.ANY)] * len(after),
        out_specs=out_specs,
        out_shape=out_shape,
        input_output_aliases=aliases or {},
        compiler_params=pltpu.CompilerParams(vmem_limit_bytes=vmem),
        cost_estimate=pl.CostEstimate(flops=flops, bytes_accessed=1000, transcendentals=0),
        name=name,
    )(*args, *after)


def pick_kernel(*refs):
    core_ref, rows_ref = refs[4:6]
    held, sems = refs[6:10], refs[10]
    copies = [pltpu.make_async_copy(refs[k], held[k], sems.at[k]) for k in range(4)]
    for copy in copies:
        copy.start()
    for copy in copies:
        copy.wait()
    tokens_ref, grad_ref, probs_ref, routes_ref = held
    count, capacity = tokens_ref.shape[0], rows_ref.shape[1]
    hit = routes_ref[...] == 0
    prob = jnp.sum(jnp.where(hit, probs_ref[...], 0.0), axis=0, keepdims=True)
    flag = jnp.max(jnp.where(hit, 1.0, 0.0), axis=0, keepdims=True)
    row = lax.broadcasted_iota(jnp.int32, (count, count), 0)
    column = lax.broadcasted_iota(jnp.int32, (count, count), 1)
    earlier = jnp.where(row < column, 1.0, 0.0).astype(jnp.bfloat16)
    flags = jnp.broadcast_to(flag, (16, count)).astype(jnp.bfloat16)
    before = jnp.dot(flags, earlier, preferred_element_type=jnp.float32)[:1]
    place = lax.broadcasted_iota(jnp.int32, (capacity, count), 0) + core_ref[0] * (capacity // 2)
    place = jnp.where(place >= capacity, place - capacity, place)
    match = (flag > 0.0) & (before.astype(jnp.int32) == place)
    picker = jnp.where(match, 1.0, 0.0).astype(jnp.bfloat16)
    scale = jnp.sum(jnp.where(match, prob, 0.0), axis=1, keepdims=True)
    rows_ref[0] = jnp.dot(picker, tokens_ref[...], preferred_element_type=jnp.float32).astype(jnp.bfloat16)
    rows_dy = jnp.dot(picker, grad_ref[...], preferred_element_type=jnp.float32)
    rows_ref[1] = (rows_dy * scale).astype(jnp.bfloat16)


def pick(tokens, out_grad, gate_probs, routes, core):
    count, width = tokens.shape
    args = (tokens, out_grad, gate_probs.T, routes.T)
    return pl.pallas_call(
        pick_kernel,
        in_specs=[pl.BlockSpec(memory_space=pltpu.HBM)] * 4 + [pl.BlockSpec(memory_space=pltpu.SMEM)],
        out_specs=pl.BlockSpec(memory_space=pltpu.VMEM),
        out_shape=jax.ShapeDtypeStruct((2, count // 4, width), jnp.bfloat16),
        scratch_shapes=[pltpu.VMEM(v.shape, v.dtype) for v in args] + [pltpu.SemaphoreType.DMA((4,))],
        compiler_params=pltpu.CompilerParams(vmem_limit_bytes=LARGE),
        cost_estimate=pl.CostEstimate(flops=1000, bytes_accessed=1000, transcendentals=0),
        name="pick",
    )(*args, core)


def own_kernel(rows_ref, w_ref, own_ref, send_ref, kept_ref, sems):
    half = own_ref.shape[1]
    steps = kept_ref.shape[1] // STEP

    def piece(i):
        here = pl.ds(pl.multiple_of(i * STEP, STEP), STEP)
        return pltpu.make_async_copy(w_ref.at[:, here, :], kept_ref.at[:, here, :], sems.at[i])

    for i in range(steps):
        piece(i).start()

    def step(i, carry):
        piece(i).wait()
        here = pl.ds(pl.multiple_of(i * STEP, STEP), STEP)
        w = kept_ref[:, here, :]
        gate_up = contract_last(rows_ref[0], w[:2].reshape(2 * STEP, w.shape[2]))
        down = contract_last(rows_ref[1], w[2])
        for m, part in enumerate((gate_up[:, :STEP], gate_up[:, STEP:], down)):
            own_ref[m, :, here] = part[:half]
            send_ref[m, :, here] = part[half:].astype(jnp.bfloat16)
        return carry

    lax.fori_loop(0, steps, step, 0)


def forward_own(rows, weights):
    half, hid = rows.shape[1] // 2, weights.shape[1]
    return pl.pallas_call(
        own_kernel,
        in_specs=[pl.BlockSpec(memory_space=pltpu.VMEM), pl.BlockSpec(memory_space=pl.ANY)],
        out_specs=[pl.BlockSpec(memory_space=pltpu.VMEM)] * 3,
        out_shape=[
            jax.ShapeDtypeStruct((3, half, hid), jnp.float32),
            jax.ShapeDtypeStruct((3, half, hid), jnp.bfloat16),
            pltpu.VMEM(weights.shape, weights.dtype),
        ],
        scratch_shapes=[pltpu.SemaphoreType.DMA((hid // STEP,))],
        compiler_params=pltpu.CompilerParams(vmem_limit_bytes=SMALL),
        cost_estimate=pl.CostEstimate(flops=1000, bytes_accessed=1000, transcendentals=0),
        name="forward_own",
    )(rows, weights)


def forward_kernel(first, top, rows_ref, w_ref, *refs):
    own_ref, send_ref = refs[-2:]
    half, step = own_ref.shape[1:]
    start = pl.multiple_of((first + pl.program_id(0)) * step, step)
    w = w_ref[:, pl.ds(start, step), :]
    gate_up = contract_last(rows_ref[0, top:, :], w[:2].reshape(2 * step, w.shape[2]))
    down = contract_last(rows_ref[1, top:, :], w[2])
    for m, part in enumerate((gate_up[:, :step], gate_up[:, step:], down)):
        own_ref[m] = part[:half]
        send_ref[m] = part[half:].astype(jnp.bfloat16)


def forward(rows, top, weights, first, steps, after):
    _, count, width = rows.shape
    half, chunk = (count - top) // 2, steps * STEP
    return call(
        functools.partial(forward_kernel, first, top),
        "forward",
        (rows, weights),
        [
            pl.BlockSpec((2, count, width), lambda i: (0, 0, 0)),
            pl.BlockSpec(memory_space=pltpu.VMEM),
        ],
        [pl.BlockSpec((3, half, STEP), lambda i: (0, 0, i))] * 2,
        [
            jax.ShapeDtypeStruct((3, half, chunk), jnp.float32),
            jax.ShapeDtypeStruct((3, half, chunk), jnp.bfloat16),
        ],
        after,
        (steps,),
        flops=FLOPS,
    )


def backward_kernel(a_ref, b_ref, c_ref, d_ref, rows_ref, *refs):
    out_ref = refs[-1]
    for m in range(3):
        parts = [ref[m].astype(jnp.float32) for ref in (a_ref, b_ref, c_ref, d_ref)]
        left = jnp.concatenate(parts, axis=0).astype(jnp.bfloat16)
        out_ref[m] = contract_first(left, rows_ref[m // 2])


def backward(lefts, rows, grads, shape, first, steps, after):
    _, count, width = rows.shape
    start, size = first * STEP, steps * STEP
    block = next(b for b in BACK_BLOCKS if start % b == 0 and size % b == 0)
    in_specs = [
        pl.BlockSpec(
            (3, v.shape[1], block),
            lambda i, k=start // block if v.shape[2] == shape[1] else 0: (0, 0, k + i),
        )
        for v in lefts
    ] + [pl.BlockSpec((2, count, width), lambda i: (0, 0, 0))]
    args, aliases = list(lefts) + [rows], {}
    if grads is not None:
        after, aliases = (grads,) + after, {len(args): 0}
    return call(
        backward_kernel,
        "backward",
        args,
        in_specs,
        pl.BlockSpec((3, block, width), lambda i: (0, start // block + i, 0)),
        jax.ShapeDtypeStruct(shape, jnp.float32),
        after,
        (size // block,),
        aliases,
        VMEM,
        BACK_FLOPS,
    )


def add_kernel(own_ref, received_ref, *refs):
    total = own_ref[...] + received_ref[...].astype(jnp.float32)
    refs[-2][...] = total
    refs[-1][...] = total.astype(jnp.bfloat16)


def act_kernel(pieces, *refs):
    left_ref, start = refs[-1], 0
    for k in range(pieces):
        total_ref, received_ref = refs[2 * k : 2 * k + 2]
        here = slice(start, start + total_ref.shape[2])
        start += total_ref.shape[2]
        gate, up, down_grad = [total_ref[m] + received_ref[m].astype(jnp.float32) for m in range(3)]
        sig = jax.nn.sigmoid(gate)
        left_ref[0, :, here] = (down_grad * up * sig * (1.0 + gate * (1.0 - sig))).astype(jnp.bfloat16)
        left_ref[1, :, here] = (down_grad * gate * sig).astype(jnp.bfloat16)
        left_ref[2, :, here] = (gate * sig * up).astype(jnp.bfloat16)


def add(own, received, after, flops=1000):
    whole = [pl.BlockSpec(memory_space=pltpu.VMEM)] * 2
    shapes = [jax.ShapeDtypeStruct(own.shape, t) for t in (jnp.float32, jnp.bfloat16)]
    return call(add_kernel, "add", (own, received), whole, whole, shapes, after, flops=flops)


def activate(sums, after):
    whole = pl.BlockSpec(memory_space=pltpu.VMEM)
    args = [v for pair in sums for v in pair]
    three, half, _ = args[0].shape
    shape = jax.ShapeDtypeStruct((three, half, sum(v.shape[2] for v, _ in sums)), jnp.bfloat16)
    kernel = functools.partial(act_kernel, len(sums))
    return call(kernel, "activate", args, [whole] * len(args), whole, shape, after)


def arrange_kernel(own_ref, lower_ref, upper_ref, far_lower_ref, far_upper_ref, *refs):
    rows_ref = refs[-1]
    half = own_ref.shape[1] // 2
    for m in range(2):
        lower, upper, one, other = [
            ref[m].astype(jnp.float32) for ref in (lower_ref, upper_ref, far_lower_ref, far_upper_ref)
        ]
        far = one + other
        parts = [own_ref[m].astype(jnp.float32), lower[:half], upper[:half], far[:half]]
        parts += [lower[half:], upper[half:], far[half:]]
        rows_ref[m] = jnp.concatenate(parts, axis=0).astype(jnp.bfloat16)


def arrange(blocks, after):
    whole = pl.BlockSpec(memory_space=pltpu.VMEM)
    two, count, width = blocks[0].shape
    shape = jax.ShapeDtypeStruct((two, 4 * count, width), jnp.bfloat16)
    return call(arrange_kernel, "arrange", blocks, [whole] * 5, whole, shape, after)


def to_core(v):
    return lax.ppermute(v, "dp", [(i, i ^ 1) for i in range(4)])


def to_chip(v):
    return lax.ppermute(v, "dp", [(i, i ^ 2) for i in range(4)])


def forward_all(rows, top, weights, chunks, last, between):
    first, firsts = 0, []
    for steps in chunks:
        firsts.append(first)
        first += steps
    parts, sums = [], []
    for k in range(len(chunks)):
        own, send = forward(rows, top, weights, firsts[k], chunks[k], last)
        parts.append((own, to_core(send)))
        last = (own,)
        if k == 0:
            left = between(last)
            last = (left,)
        for ready in ([0] if k == 0 else [k - 1] if k >= 2 else []):
            total, sent = add(*parts[ready], last)
            sums.append((total, to_chip(sent)))
            last = (total,)
    return sums, parts[-1], left, last


def pipeline(block, weights):
    lower = lax.ppermute(block, "expert", [(i, (i + 1) % 4) for i in range(4)])
    upper = lax.ppermute(block, "expert", [(i, (i - 1) % 4) for i in range(4)])
    own, send, resident = forward_own(block, weights)
    lower_out, _ = lax.optimization_barrier((lower, own))
    far_lower = lax.ppermute(lower_out, "expert", [(1, 2), (2, 3)])
    far_upper = lax.ppermute(upper, "expert", [(2, 1), (1, 0)])
    total, sent = add(own, to_core(send), ())
    own_sums, last = [(total, to_chip(sent))], (total,)
    rows = arrange([block, lower, upper, far_lower, far_upper], last)
    sums, final, left, last = forward_all(
        rows, block.shape[1], resident, REST_CHUNKS, (rows,), functools.partial(activate, own_sums)
    )
    own_left = [left, to_core(left)]
    firsts = [sum(REST_CHUNKS[:k]) for k in range(len(REST_CHUNKS))]
    grads, lefts = None, []
    for k, ahead in enumerate(AHEAD):
        while len(lefts) < ahead:
            left = activate([sums[len(lefts)]], last)
            lefts.append([left, to_core(left)])
            last = (left,)
            if len(lefts) == DEFER:
                total, sent = add(*final, last, FINAL_FLOPS)
                sums.append((total, to_chip(sent)))
                last = (total,)
        after = () if grads is not None and last[0] is grads else last
        grads = backward(
            own_left + lefts[k], rows, grads, weights.shape, firsts[k], REST_CHUNKS[k], after
        )
        last = (grads,)
    return grads


def fallback(block, weights):
    moved = lax.all_gather(block, "expert", axis=1, tiled=True)
    _, hid, width = weights.shape
    gate_up = contract_last(moved[0], weights[:2].reshape(2 * hid, width))
    down = contract_last(moved[1], weights[2])
    total = lax.psum(jnp.concatenate([gate_up, down], axis=1), "dp")
    left = activations(total[:, :hid], total[:, hid : 2 * hid], total[:, 2 * hid :])
    return jnp.stack(
        [
            contract_first(left[0], moved[0]),
            contract_first(left[1], moved[0]),
            contract_first(left[2], moved[1]),
        ]
    )


def per_device(n_expert, n_dp, tokens, out_grad, gate_probs, routes, weights):
    hid = weights.shape[1]
    if n_expert == 4 and n_dp == 4 and hid == STEP * sum(REST_CHUNKS) and tokens.shape[0] % 64 == 0:
        core = lax.rem(lax.axis_index("dp"), 2).reshape(1)
        return pipeline(pick(tokens, out_grad, gate_probs, routes, core), weights)
    return fallback(pick_rows(tokens, out_grad, gate_probs, routes), weights)


def solution(mesh):
    in_specs = (
        P(("group", "expert"), "dp"),
        P(("group", "expert"), "dp"),
        P(("group", "expert"), None),
        P(("group", "expert"), None),
        P(None, "expert", "dp"),
    )
    out_specs = P("group", "expert", "dp")
    step = functools.partial(per_device, mesh.shape["expert"], mesh.shape["dp"])
    return jax.shard_map(
        step, mesh=mesh, in_specs=in_specs, out_specs=out_specs, check_vma=False
    )
```

```python
import functools

import jax
import jax.numpy as jnp
from jax import lax
from jax.experimental import pallas as pl
from jax.experimental.pallas import tpu as pltpu
from jax.sharding import PartitionSpec as P

STEP = 384
BACK_BLOCKS = (256, 128)
REST_CHUNKS = (2, 2, 2, 1)
AHEAD = (1, 2, 4, 4)
DEFER = 1
FENCES = (0, 1, 2)
VMEM = 24 * 1024 * 1024
SMALL = 8 * 1024 * 1024
LARGE = 253 * 256 * 1024
FLOPS = 4 * 10**9
BACK_FLOPS = 1000
FINAL_FLOPS = 5*10**9


def contract_last(left, right):
    return lax.dot_general(
        left, right, (((1,), (1,)), ((), ())), preferred_element_type=jnp.float32
    )


def contract_first(left, right):
    return lax.dot_general(
        left, right, (((0,), (0,)), ((), ())), preferred_element_type=jnp.float32
    )


def activations(gate, up, down_grad):
    sig = jax.nn.sigmoid(gate)
    hidden = gate * sig * up
    gate_grad = down_grad * up * sig * (1.0 + gate * (1.0 - sig))
    up_grad = down_grad * gate * sig
    return jnp.stack([gate_grad, up_grad, hidden]).astype(jnp.bfloat16)


def pick_rows(tokens, out_grad, gate_probs, routes):
    capacity = tokens.shape[0] // 4
    hit = routes == 0
    token_hit = jnp.any(hit, axis=1)
    prob = jnp.sum(jnp.where(hit, gate_probs, jnp.zeros_like(gate_probs)), axis=1)
    flags = token_hit.astype(jnp.int32)
    before = jnp.cumsum(flags, dtype=jnp.int32) - flags
    place = jnp.arange(capacity, dtype=jnp.int32)
    match = token_hit[None, :] & (before[None, :] == place[:, None])
    picker = match.astype(jnp.bfloat16)
    scaled = (out_grad.astype(jnp.float32) * prob[:, None]).astype(jnp.bfloat16)
    rows_x = jnp.dot(picker, tokens, preferred_element_type=jnp.float32).astype(jnp.bfloat16)
    rows_dy = jnp.dot(picker, scaled, preferred_element_type=jnp.float32).astype(jnp.bfloat16)
    return jnp.stack([rows_x, rows_dy])


def call(kernel, name, args, in_specs, out_specs, out_shape, after=(), grid=(), aliases=None, vmem=SMALL, flops=1000):
    return pl.pallas_call(
        kernel,
        grid=grid,
        in_specs=list(in_specs) + [pl.BlockSpec(memory_space=pl.ANY)] * len(after),
        out_specs=out_specs,
        out_shape=out_shape,
        input_output_aliases=aliases or {},
        compiler_params=pltpu.CompilerParams(vmem_limit_bytes=vmem),
        cost_estimate=pl.CostEstimate(flops=flops, bytes_accessed=1000, transcendentals=0),
        name=name,
    )(*args, *after)


def pick_kernel(*refs):
    core_ref, rows_ref = refs[4:6]
    held, sems = refs[6:10], refs[10]
    copies = [pltpu.make_async_copy(refs[k], held[k], sems.at[k]) for k in range(4)]
    for copy in copies:
        copy.start()
    for copy in copies:
        copy.wait()
    tokens_ref, grad_ref, probs_ref, routes_ref = held
    count, capacity = tokens_ref.shape[0], rows_ref.shape[1]
    hit = routes_ref[...] == 0
    prob = jnp.sum(jnp.where(hit, probs_ref[...], 0.0), axis=0, keepdims=True)
    flag = jnp.max(jnp.where(hit, 1.0, 0.0), axis=0, keepdims=True)
    row = lax.broadcasted_iota(jnp.int32, (count, count), 0)
    column = lax.broadcasted_iota(jnp.int32, (count, count), 1)
    earlier = jnp.where(row < column, 1.0, 0.0).astype(jnp.bfloat16)
    flags = jnp.broadcast_to(flag, (16, count)).astype(jnp.bfloat16)
    before = jnp.dot(flags, earlier, preferred_element_type=jnp.float32)[:1]
    place = lax.broadcasted_iota(jnp.int32, (capacity, count), 0) + core_ref[0] * (capacity // 2)
    place = jnp.where(place >= capacity, place - capacity, place)
    match = (flag > 0.0) & (before.astype(jnp.int32) == place)
    picker = jnp.where(match, 1.0, 0.0).astype(jnp.bfloat16)
    scale = jnp.sum(jnp.where(match, prob, 0.0), axis=1, keepdims=True)
    rows_ref[0] = jnp.dot(picker, tokens_ref[...], preferred_element_type=jnp.float32).astype(jnp.bfloat16)
    rows_dy = jnp.dot(picker, grad_ref[...], preferred_element_type=jnp.float32)
    rows_ref[1] = (rows_dy * scale).astype(jnp.bfloat16)


def pick(tokens, out_grad, gate_probs, routes, core):
    count, width = tokens.shape
    args = (tokens, out_grad, gate_probs.T, routes.T)
    return pl.pallas_call(
        pick_kernel,
        in_specs=[pl.BlockSpec(memory_space=pltpu.HBM)] * 4 + [pl.BlockSpec(memory_space=pltpu.SMEM)],
        out_specs=pl.BlockSpec(memory_space=pltpu.VMEM),
        out_shape=jax.ShapeDtypeStruct((2, count // 4, width), jnp.bfloat16),
        scratch_shapes=[pltpu.VMEM(v.shape, v.dtype) for v in args] + [pltpu.SemaphoreType.DMA((4,))],
        compiler_params=pltpu.CompilerParams(vmem_limit_bytes=LARGE),
        cost_estimate=pl.CostEstimate(flops=1000, bytes_accessed=1000, transcendentals=0),
        name="pick",
    )(*args, core)


def own_kernel(rows_ref, w_ref, own_ref, send_ref, kept_ref, sems):
    half = own_ref.shape[1]
    steps = kept_ref.shape[1] // STEP

    def piece(i):
        here = pl.ds(pl.multiple_of(i * STEP, STEP), STEP)
        return pltpu.make_async_copy(w_ref.at[:, here, :], kept_ref.at[:, here, :], sems.at[i])

    for i in range(steps):
        piece(i).start()

    def step(i, carry):
        piece(i).wait()
        here = pl.ds(pl.multiple_of(i * STEP, STEP), STEP)
        w = kept_ref[:, here, :]
        gate_up = contract_last(rows_ref[0], w[:2].reshape(2 * STEP, w.shape[2]))
        down = contract_last(rows_ref[1], w[2])
        for m, part in enumerate((gate_up[:, :STEP], gate_up[:, STEP:], down)):
            own_ref[m, :, here] = part[:half]
            send_ref[m, :, here] = part[half:].astype(jnp.bfloat16)
        return carry

    lax.fori_loop(0, steps, step, 0)


def forward_own(rows, weights):
    half, hid = rows.shape[1] // 2, weights.shape[1]
    return pl.pallas_call(
        own_kernel,
        in_specs=[pl.BlockSpec(memory_space=pltpu.VMEM), pl.BlockSpec(memory_space=pl.ANY)],
        out_specs=[pl.BlockSpec(memory_space=pltpu.VMEM)] * 3,
        out_shape=[
            jax.ShapeDtypeStruct((3, half, hid), jnp.float32),
            jax.ShapeDtypeStruct((3, half, hid), jnp.bfloat16),
            pltpu.VMEM(weights.shape, weights.dtype),
        ],
        scratch_shapes=[pltpu.SemaphoreType.DMA((hid // STEP,))],
        compiler_params=pltpu.CompilerParams(vmem_limit_bytes=SMALL),
        cost_estimate=pl.CostEstimate(flops=1000, bytes_accessed=1000, transcendentals=0),
        name="forward_own",
    )(rows, weights)


def forward_kernel(first, top, rows_ref, w_ref, *refs):
    own_ref, send_ref = refs[-2:]
    half, step = own_ref.shape[1:]
    start = pl.multiple_of((first + pl.program_id(0)) * step, step)
    w = w_ref[:, pl.ds(start, step), :]
    gate_up = contract_last(rows_ref[0, top:, :], w[:2].reshape(2 * step, w.shape[2]))
    down = contract_last(rows_ref[1, top:, :], w[2])
    for m, part in enumerate((gate_up[:, :step], gate_up[:, step:], down)):
        own_ref[m] = part[:half]
        send_ref[m] = part[half:].astype(jnp.bfloat16)


def forward(rows, top, weights, first, steps, after):
    _, count, width = rows.shape
    half, chunk = (count - top) // 2, steps * STEP
    return call(
        functools.partial(forward_kernel, first, top),
        "forward",
        (rows, weights),
        [
            pl.BlockSpec((2, count, width), lambda i: (0, 0, 0)),
            pl.BlockSpec(memory_space=pltpu.VMEM),
        ],
        [pl.BlockSpec((3, half, STEP), lambda i: (0, 0, i))] * 2,
        [
            jax.ShapeDtypeStruct((3, half, chunk), jnp.float32),
            jax.ShapeDtypeStruct((3, half, chunk), jnp.bfloat16),
        ],
        after,
        (steps,),
        flops=FLOPS,
    )


def backward_kernel(a_ref, b_ref, c_ref, d_ref, rows_ref, *refs):
    out_ref = refs[-1]
    for m in range(3):
        parts = [ref[m].astype(jnp.float32) for ref in (a_ref, b_ref, c_ref, d_ref)]
        left = jnp.concatenate(parts, axis=0).astype(jnp.bfloat16)
        out_ref[m] = contract_first(left, rows_ref[m // 2])


def backward(lefts, rows, grads, shape, first, steps, after):
    _, count, width = rows.shape
    start, size = first * STEP, steps * STEP
    block = next(b for b in BACK_BLOCKS if start % b == 0 and size % b == 0)
    in_specs = [
        pl.BlockSpec(
            (3, v.shape[1], block),
            lambda i, k=start // block if v.shape[2] == shape[1] else 0: (0, 0, k + i),
        )
        for v in lefts
    ] + [pl.BlockSpec((2, count, width), lambda i: (0, 0, 0))]
    args, aliases = list(lefts) + [rows], {}
    if grads is not None:
        after, aliases = (grads,) + after, {len(args): 0}
    return call(
        backward_kernel,
        "backward",
        args,
        in_specs,
        pl.BlockSpec((3, block, width), lambda i: (0, start // block + i, 0)),
        jax.ShapeDtypeStruct(shape, jnp.float32),
        after,
        (size // block,),
        aliases,
        VMEM,
        BACK_FLOPS,
    )


def add_kernel(own_ref, received_ref, *refs):
    total = own_ref[...] + received_ref[...].astype(jnp.float32)
    refs[-2][...] = total
    refs[-1][...] = total.astype(jnp.bfloat16)


def act_kernel(pieces, *refs):
    left_ref, start = refs[-1], 0
    for k in range(pieces):
        total_ref, received_ref = refs[2 * k : 2 * k + 2]
        here = slice(start, start + total_ref.shape[2])
        start += total_ref.shape[2]
        gate, up, down_grad = [total_ref[m] + received_ref[m].astype(jnp.float32) for m in range(3)]
        sig = jax.nn.sigmoid(gate)
        left_ref[0, :, here] = (down_grad * up * sig * (1.0 + gate * (1.0 - sig))).astype(jnp.bfloat16)
        left_ref[1, :, here] = (down_grad * gate * sig).astype(jnp.bfloat16)
        left_ref[2, :, here] = (gate * sig * up).astype(jnp.bfloat16)


def add(own, received, after, flops=1000):
    whole = [pl.BlockSpec(memory_space=pltpu.VMEM)] * 2
    shapes = [jax.ShapeDtypeStruct(own.shape, t) for t in (jnp.float32, jnp.bfloat16)]
    return call(add_kernel, "add", (own, received), whole, whole, shapes, after, flops=flops)


def activate(sums, after):
    whole = pl.BlockSpec(memory_space=pltpu.VMEM)
    args = [v for pair in sums for v in pair]
    three, half, _ = args[0].shape
    shape = jax.ShapeDtypeStruct((three, half, sum(v.shape[2] for v, _ in sums)), jnp.bfloat16)
    kernel = functools.partial(act_kernel, len(sums))
    return call(kernel, "activate", args, [whole] * len(args), whole, shape, after)


def arrange_kernel(own_ref, lower_ref, upper_ref, far_lower_ref, far_upper_ref, *refs):
    rows_ref = refs[-1]
    half = own_ref.shape[1] // 2
    for m in range(2):
        lower, upper, one, other = [
            ref[m].astype(jnp.float32) for ref in (lower_ref, upper_ref, far_lower_ref, far_upper_ref)
        ]
        far = one + other
        parts = [own_ref[m].astype(jnp.float32), lower[:half], upper[:half], far[:half]]
        parts += [lower[half:], upper[half:], far[half:]]
        rows_ref[m] = jnp.concatenate(parts, axis=0).astype(jnp.bfloat16)


def arrange(blocks, after):
    whole = pl.BlockSpec(memory_space=pltpu.VMEM)
    two, count, width = blocks[0].shape
    shape = jax.ShapeDtypeStruct((two, 4 * count, width), jnp.bfloat16)
    return call(arrange_kernel, "arrange", blocks, [whole] * 5, whole, shape, after)


def fence_kernel(*refs):
    refs[-1][...] = jnp.zeros(refs[-1].shape, jnp.float32)


def fence(after):
    whole = pl.BlockSpec(memory_space=pltpu.VMEM)
    shape = jax.ShapeDtypeStruct((8, 128), jnp.float32)
    return call(fence_kernel, "fence", (), [], whole, shape, after, flops=FINAL_FLOPS)


def to_core(v):
    return lax.ppermute(v, "dp", [(i, i ^ 1) for i in range(4)])


def to_chip(v):
    return lax.ppermute(v, "dp", [(i, i ^ 2) for i in range(4)])


def forward_all(rows, top, weights, chunks, last, between):
    first, firsts = 0, []
    for steps in chunks:
        firsts.append(first)
        first += steps
    parts, sums = [], []
    for k in range(len(chunks)):
        own, send = forward(rows, top, weights, firsts[k], chunks[k], last)
        parts.append((own, to_core(send)))
        last = (own,)
        if k == 0:
            left = between(last)
            last = (left,)
        for ready in ([0] if k == 0 else [k - 1] if k >= 2 else []):
            total, sent = add(*parts[ready], last)
            sums.append((total, to_chip(sent)))
            last = (total,)
    return sums, parts[-1], left, last


def pipeline(block, weights):
    lower = lax.ppermute(block, "expert", [(i, (i + 1) % 4) for i in range(4)])
    upper = lax.ppermute(block, "expert", [(i, (i - 1) % 4) for i in range(4)])
    own, send, resident = forward_own(block, weights)
    lower_out, _ = lax.optimization_barrier((lower, own))
    far_lower = lax.ppermute(lower_out, "expert", [(1, 2), (2, 3)])
    far_upper = lax.ppermute(upper, "expert", [(2, 1), (1, 0)])
    total, sent = add(own, to_core(send), ())
    own_sums, last = [(total, to_chip(sent))], (total,)
    rows = arrange([block, lower, upper, far_lower, far_upper], last)
    sums, final, left, last = forward_all(
        rows, block.shape[1], resident, REST_CHUNKS, (rows,), functools.partial(activate, own_sums)
    )
    own_left = [left, to_core(left)]
    firsts = [sum(REST_CHUNKS[:k]) for k in range(len(REST_CHUNKS))]
    grads, lefts = None, []
    for k, ahead in enumerate(AHEAD):
        while len(lefts) < ahead:
            left = activate([sums[len(lefts)]], last)
            lefts.append([left, to_core(left)])
            last = (left,)
            if len(lefts) == DEFER:
                total, sent = add(*final, last, FINAL_FLOPS)
                sums.append((total, to_chip(sent)))
                last = (total,)
        if k in FENCES:
            last = (fence(last),)
        after = () if grads is not None and last[0] is grads else last
        grads = backward(
            own_left + lefts[k], rows, grads, weights.shape, firsts[k], REST_CHUNKS[k], after
        )
        last = (grads,)
    return grads


def fallback(block, weights):
    moved = lax.all_gather(block, "expert", axis=1, tiled=True)
    _, hid, width = weights.shape
    gate_up = contract_last(moved[0], weights[:2].reshape(2 * hid, width))
    down = contract_last(moved[1], weights[2])
    total = lax.psum(jnp.concatenate([gate_up, down], axis=1), "dp")
    left = activations(total[:, :hid], total[:, hid : 2 * hid], total[:, 2 * hid :])
    return jnp.stack(
        [
            contract_first(left[0], moved[0]),
            contract_first(left[1], moved[0]),
            contract_first(left[2], moved[1]),
        ]
    )


def per_device(n_expert, n_dp, tokens, out_grad, gate_probs, routes, weights):
    hid = weights.shape[1]
    if n_expert == 4 and n_dp == 4 and hid == STEP * sum(REST_CHUNKS) and tokens.shape[0] % 64 == 0:
        core = lax.rem(lax.axis_index("dp"), 2).reshape(1)
        return pipeline(pick(tokens, out_grad, gate_probs, routes, core), weights)
    return fallback(pick_rows(tokens, out_grad, gate_probs, routes), weights)


def solution(mesh):
    in_specs = (
        P(("group", "expert"), "dp"),
        P(("group", "expert"), "dp"),
        P(("group", "expert"), None),
        P(("group", "expert"), None),
        P(None, "expert", "dp"),
    )
    out_specs = P("group", "expert", "dp")
    step = functools.partial(per_device, mesh.shape["expert"], mesh.shape["dp"])
    return jax.shard_map(
        step, mesh=mesh, in_specs=in_specs, out_specs=out_specs, check_vma=False
    )
```
